768 devices in a mesh: rows: 48 (over x, z), inner: 16 (over y, core).
Axes of the slice: x: 4, y: 8, z: 12, core: 2. Of those that a mesh axis runs over, the one named last changes fastest.
Arguments:
- factor: bfloat16 [96, 16, 128, 128], P('rows'), may hold values from -1.1953125 to 1.1953125
- target_blocks: bfloat16 [96, 16, 128, 128], P('rows', 'inner'), may hold values from -6 to 6
- diag_inverse: bfloat16 [96, 128, 128], P('rows'), may hold values from -0.5 to 0.5
- cols: int32 [96, 16], P('rows'), may hold values from -1 to 94, as said below
- pair_list: int32 [3, 48, 16, 16, 2], P(None, 'rows', 'inner'), may hold values from 0 to 15, as said below
Outputs:
- new_factor: bfloat16 [96, 16, 128, 128], P('rows', 'inner')
The draws below stay inside these ranges and needn't reach their ends.
Inputs may be any that keep to these rules, and one draw needn't show every extreme that they name: cols[i, b] lies in i - 16 to i - 1 and is not below -1; only row 0 holds -1. `pair_list`: field 0 lies in 0 to 1, field 1 in 0 to 15, field 2 is 0 or 1; slots with flag 0 carry no pair.
All inputs are finite; a program needn't handle non-finite values.
Results may differ from the reference program's by a relative error of at most 0.014.
Values may be sent and summed in bfloat16 or wider, within the bound.
A program may use at most 32 MiB of HBM per device.

```python
import jax
import jax.numpy as jnp
from jax import lax

BS = 128
R_DEV = 2
BAND = 16
SLOTS = 2
NB = 16
ROWS = 96
ROW_DEVS = 48
INNERS = 16


def draw_cols(key, part):
    key = jax.random.fold_in(key, 11)
    offsets = jax.random.randint(key, (ROWS, NB), 0, BAND, dtype=jnp.int32)
    row_ids = jnp.arange(ROWS, dtype=jnp.int32)[:, None]
    return row_ids - 1 - offsets % jnp.maximum(row_ids, 1)


def draw_pair_list(key, part):
    key = jax.random.fold_in(key, 23)
    key_rows, key_slots, key_live = jax.random.split(key, 3)
    shape = (ROW_DEVS, INNERS, NB, SLOTS)
    row_local = jax.random.randint(key_rows, shape, 0, R_DEV, dtype=jnp.int32)
    left_slot = jax.random.randint(key_slots, shape, 0, NB, dtype=jnp.int32)
    live_flag = jnp.minimum(jax.random.randint(key_live, shape, 0, 4, dtype=jnp.int32), 1)
    return jnp.stack([row_local, left_slot, live_flag], 0)


def level_of(rng, dims, cuts, low, largest):
    loudness, own = 1.0, jax.random.fold_in(rng, 6)
    for position, blocks in cuts:
        heights = jnp.exp(jax.random.uniform(jax.random.fold_in(own, position), (blocks,), jnp.float32, low / len(cuts), largest / len(cuts)))
        loudness = loudness * jnp.repeat(heights, dims[position] // blocks).reshape([-1 if axis == position else 1 for axis in range(len(dims))])
    return loudness


def centred(own_key, dims, deviation, limit, pieces=(), kind=jnp.bfloat16):
    entries = deviation * jax.random.normal(own_key, dims, jnp.float32)
    if pieces:
        entries = entries * level_of(own_key, dims, pieces, -0.22, 0.18)
    return jnp.clip(entries, -limit, limit).astype(kind)


def setup_inputs(seed: int = 0) -> dict:
    key_of = jax.random.split(jax.random.key(seed), 6)
    factor = centred(key_of[0], (ROWS, NB, BS, BS), 0.2, 1.1953125, ((0, 48),))
    target_blocks = centred(key_of[1], (ROWS, NB, BS, BS), 1.0, 6.0, ((0, 48), (1, 16)))
    diag_inverse = centred(key_of[2], (ROWS, BS, BS), BS ** -0.5, 0.5, ((0, 48),))
    cols = draw_cols(jax.random.fold_in(key_of[5], 71), 0)
    pair_list = draw_pair_list(jax.random.fold_in(key_of[5], 71), 0)
    return {"factor": factor, "target_blocks": target_blocks, "diag_inverse": diag_inverse, "cols": cols, "pair_list": pair_list}


def reference(factor, target_blocks, diag_inverse, cols, pair_list):
    padded_factor = jnp.concatenate([jnp.zeros((BAND, NB, BS, BS), jnp.bfloat16), factor], 0)
    padded_inverse = jnp.concatenate([jnp.zeros((BAND, BS, BS), jnp.bfloat16), diag_inverse], 0)
    group_rows = jnp.arange(R_DEV, dtype=jnp.int32)
    slot_ids = jnp.arange(NB, dtype=jnp.int32)
    inner_ids = jnp.arange(INNERS, dtype=jnp.int32)

    def one_group(group_index):
        pair_fields = lax.dynamic_index_in_dim(pair_list, group_index, 1, keepdims=False)
        row_local = pair_fields[0]
        left_slot = pair_fields[1]
        live_flag = pair_fields[2]
        first_row = group_index * R_DEV
        rows_of = first_row + row_local
        columns = cols[rows_of, slot_ids[None, :, None]]
        left_blocks = factor[rows_of, left_slot].astype(jnp.float32)
        right_blocks = padded_factor[columns + BAND, inner_ids[:, None, None]].astype(jnp.float32)
        products = jnp.einsum('dbsxk,dbsyk->dbsxy', left_blocks, right_blocks)
        weights = ((row_local[..., None] == group_rows) & (live_flag[..., None] == 1)).astype(jnp.float32)
        partial_sums = jnp.einsum('dbsi,dbsxy->ibxy', weights, products)
        own_blocks = lax.dynamic_slice_in_dim(target_blocks, first_row, R_DEV, 0).astype(jnp.float32)
        difference = (own_blocks - partial_sums).astype(jnp.bfloat16)
        own_cols = lax.dynamic_slice_in_dim(cols, first_row, R_DEV, 0)
        inverses = padded_inverse[own_cols + BAND].astype(jnp.float32)
        return jnp.einsum('ibxk,ibky->ibxy', difference.astype(jnp.float32), inverses).astype(jnp.bfloat16)

    result = lax.map(one_group, jnp.arange(ROW_DEVS, dtype=jnp.int32))
    return result.reshape(ROWS, NB, BS, BS)
```

```python
import jax
import jax.numpy as jnp
from jax import lax
from jax.experimental import pallas as pl
from jax.experimental.pallas import tpu as pltpu
from jax.sharding import PartitionSpec as P

MESH = pl.DeviceIdType.MESH
BAND = 16
BS = 128
GROUPS = 48
RING = 8
HOPS = 8
SLICE = 16
BLOCK = 2 * BS + 2 * SLICE
WINDOW = ((0, 2), (0, 8), (0, 1), (2, 4), (2, 3), (8, 7), (4, 5), (7, 6))
STEPS = tuple(sorted({m - k for k, m in WINDOW}))
EDGE_OF = {m: n for n, (k, m) in enumerate(WINDOW)}
ROUND = tuple(range(1, RING))
ORDER = (3, 5, 4, 1, 7, 2, 6, 0)


def kernel(
    factor, target, inverse, cols, pairs, out,
    left, own, mate, mate_pairs, part, far, inv_out, inv_in, near, goal,
    local_sem, win_send, win_recv, mate_send, mate_recv, list_send, list_recv,
    sum_send, sum_recv, inv_send, inv_recv,
):
    group = lax.axis_index("rows")
    slot = lax.axis_index("inner")
    ring_at = slot // 2
    core = slot % 2
    other = slot + 1 - 2 * core
    first_row = group * 2 - BAND

    def along(step):
        return (lax.rem(group + step + GROUPS, GROUPS), slot)

    def around(step):
        return (group, lax.rem(ring_at + step + RING, RING) * 2 + core)

    sibling = (group, other)

    loads = [
        pltpu.make_async_copy(factor.at[:, slot], own.at[0, :, pl.ds(0, BS)], local_sem.at[0]),
        pltpu.make_async_copy(
            inverse.at[:, pl.ds(pl.multiple_of(ring_at * SLICE, SLICE), SLICE)],
            own.at[0, :, pl.ds(BS, SLICE)],
            local_sem.at[1],
        ),
        pltpu.make_async_copy(factor.at[:, other], mate.at[0], local_sem.at[2]),
        pltpu.make_async_copy(factor, left, local_sem.at[3]),
        pltpu.make_async_copy(target, goal, local_sem.at[4]),
    ]
    for load in loads:
        load.start()

    barrier = pltpu.get_barrier_semaphore()
    for step in STEPS:
        pl.semaphore_signal(barrier, inc=1, device_id=along(-step), device_id_type=MESH)
    for step in ROUND:
        pl.semaphore_signal(barrier, inc=1, device_id=around(-step), device_id_type=MESH)
    pl.semaphore_signal(barrier, inc=1, device_id=sibling, device_id_type=MESH)
    loads[0].wait()
    loads[1].wait()
    pl.semaphore_wait(barrier, len(STEPS) + len(ROUND) + 1)

    def remote(source, destination, send_sem, recv_sem, device):
        return pltpu.make_async_remote_copy(
            src_ref=source, dst_ref=destination, send_sem=send_sem, recv_sem=recv_sem,
            device_id=device, device_id_type=MESH,
        )

    sent = []

    def send(*where):
        copy = remote(*where)
        copy.start()
        sent.append(copy)

    def window_copy(n):
        k, m = WINDOW[n]
        return own.at[k], own.at[m], win_send.at[n], win_recv.at[n], along(m - k)

    def mate_copy(k):
        return own.at[k, :, pl.ds(0, BS)], mate.at[k], mate_send.at[k - 1], mate_recv.at[k - 1], sibling

    for n, (k, m) in enumerate(WINDOW):
        if k == 0:
            send(*window_copy(n))
    list_copy = (pairs, mate_pairs, list_send.at[0], list_recv.at[0], sibling)
    send(*list_copy)
    for arrival, (_, held) in enumerate(WINDOW):
        remote(*window_copy(arrival)).wait_recv()
        for n, (k, m) in enumerate(WINDOW):
            if k == held:
                send(*window_copy(n))
        send(*mate_copy(held))
    for load in loads[2:]:
        load.wait()
    remote(*list_copy).wait_recv()
    for _, held in WINDOW:
        remote(*mate_copy(held)).wait_recv()

    def locate(row, column):
        relative = cols[row, column] - first_row
        back = HOPS - lax.shift_right_arithmetic(relative, 1)
        return jnp.clip(back, 0, HOPS), relative & 1

    def partial_sums(e):
        column = lax.rem(ring_at + e, RING) * 2 + core
        totals = [jnp.zeros((BS, BS), jnp.float32) for _ in range(2)]
        for table, window in ((pairs, own), (mate_pairs, mate)):
            for s in range(2):
                row = table[0, 0, 0, s, column]
                a = table[1, 0, 0, s, column]
                live = table[2, 0, 0, s, column]
                back, half = locate(row, column)
                product = lax.dot_general(
                    left[row, a], window[back, half, pl.ds(0, BS)],
                    (((1,), (1,)), ((), ())), preferred_element_type=jnp.float32,
                )
                for i in range(2):
                    wanted = jnp.logical_and(live == 1, row == i)
                    totals[i] = totals[i] + jnp.where(wanted, product, 0.0)
        return totals

    def hold(e):
        for i, total in enumerate(partial_sums(e)):
            part[e, i] = total.astype(jnp.bfloat16)

    def sum_copy(n):
        source, destination, step = {
            0: (part.at[3], near.at[0], 1),
            1: (part.at[5], near.at[1], -1),
            2: (part.at[4, 0], far.at[0], -2),
            3: (part.at[4, 1], far.at[1], 2),
            4: (part.at[1], near.at[2], 1),
            5: (part.at[7], near.at[3], -1),
            6: (part.at[2], near.at[4], 2),
            7: (part.at[6], near.at[5], -2),
        }[n]
        return source, destination, sum_send.at[n], sum_recv.at[n], around(step)

    def inverse_copy(e):
        place = pl.ds(pl.multiple_of(ring_at * SLICE, SLICE), SLICE)
        return inv_out.at[e], inv_in.at[:, place], inv_send.at[e - 1], inv_recv.at[e - 1], around(e)

    hold(3)
    send(*sum_copy(0))
    hold(5)
    send(*sum_copy(1))
    hold(4)
    send(*sum_copy(2))
    send(*sum_copy(3))
    for e in (4, 3, 5, 2, 6, 1, 7, 0):
        column = lax.rem(ring_at + e, RING) * 2 + core
        for i in range(2):
            back, half = locate(i, column)
            inv_out[e, i] = own[back, half, pl.ds(BS, SLICE)]
        if e:
            send(*inverse_copy(e))
    hold(1)
    send(*sum_copy(4))
    hold(7)
    send(*sum_copy(5))
    for e, n, first, second, extra_row, extra in ((2, 6, 0, 3, 1, 1), (6, 7, 1, 2, 0, 0)):
        totals = partial_sums(e)
        remote(*sum_copy(first)).wait_recv()
        remote(*sum_copy(second)).wait_recv()
        for i in range(2):
            total = totals[i] + near[first, i].astype(jnp.float32)
            if i == extra_row:
                total = total + far[extra].astype(jnp.float32)
            part[e, i] = total.astype(jnp.bfloat16)
        send(*sum_copy(n))
    totals = partial_sums(0)
    inv_in[:, pl.ds(pl.multiple_of(ring_at * SLICE, SLICE), SLICE), :] = inv_out[0]
    for n in (4, 5, 6, 7):
        remote(*sum_copy(n)).wait_recv()
        for i in range(2):
            totals[i] = totals[i] + near[n - 2, i].astype(jnp.float32)
    for e in ROUND:
        place = pl.ds(pl.multiple_of(lax.rem(ring_at - e + RING, RING) * SLICE, SLICE), SLICE)
        remote(
            inv_out.at[e], inv_in.at[:, place], inv_send.at[e - 1], inv_recv.at[e - 1], around(e)
        ).wait_recv()
    for i in range(2):
        difference = (goal[i, 0].astype(jnp.float32) - totals[i]).astype(jnp.bfloat16)
        result = jnp.dot(difference, inv_in[i], preferred_element_type=jnp.float32)
        result = jnp.where(cols[i, slot] < 0, 0.0, result)
        out[i, 0] = result.astype(jnp.bfloat16)
    for copy in sent:
        copy.wait_send()


def per_device(factor, target_blocks, diag_inverse, cols, pair_list):
    bf16 = jnp.bfloat16
    anywhere = pl.BlockSpec(memory_space=pltpu.HBM)
    scalars = pl.BlockSpec(memory_space=pltpu.SMEM)
    dma = pltpu.SemaphoreType.DMA
    return pl.pallas_call(
        kernel,
        out_shape=jax.ShapeDtypeStruct((2, 1, BS, BS), bf16),
        in_specs=[anywhere, anywhere, anywhere, scalars, scalars],
        out_specs=pl.BlockSpec(memory_space=pltpu.VMEM),
        scratch_shapes=[
            pltpu.VMEM((2, 16, BS, BS), bf16),
            pltpu.VMEM((HOPS + 1, 2, BS + SLICE, BS), bf16),
            pltpu.VMEM((HOPS + 1, 2, BS, BS), bf16),
            pltpu.SMEM((3, 1, 1, 2, 16), jnp.int32),
            pltpu.VMEM((RING, 2, BS, BS), bf16),
            pltpu.VMEM((2, BS, BS), bf16),
            pltpu.VMEM((RING, 2, SLICE, BS), bf16),
            pltpu.VMEM((2, BS, BS), bf16),
            pltpu.VMEM((6, 2, BS, BS), bf16),
            pltpu.VMEM((2, 1, BS, BS), bf16),
            dma((5,)),
            dma((len(WINDOW),)),
            dma((len(WINDOW),)),
            dma((HOPS,)),
            dma((HOPS,)),
            dma((1,)),
            dma((1,)),
            dma((8,)),
            dma((8,)),
            dma((RING - 1,)),
            dma((RING - 1,)),
        ],
        compiler_params=pltpu.CompilerParams(
            collective_id=0, has_side_effects=True, vmem_limit_bytes=60 * 1024 * 1024
        ),
        name="sweep",
    )(factor, target_blocks, diag_inverse, cols, jnp.swapaxes(pair_list, 3, 4))


def solution(mesh):
    placed = (
        P("rows", None, None, None),
        P("rows", "inner", None, None),
        P("rows", None, None),
        P("rows", None),
        P(None, "rows", "inner", None, None),
    )
    return jax.shard_map(
        per_device,
        mesh=mesh,
        in_specs=placed,
        out_specs=P("rows", "inner", None, None),
        check_vma=False,
    )
```

```python
import jax
import jax.numpy as jnp
from jax import lax
from jax.experimental import pallas as pl
from jax.experimental.pallas import tpu as pltpu
from jax.sharding import PartitionSpec as P

MESH = pl.DeviceIdType.MESH
BAND = 16
BS = 128
GROUPS = 48
RING = 8
HOPS = 8
SLICE = 16
WINDOW = ((0, 2), (0, 8), (0, 1), (2, 4), (2, 3), (8, 7), (4, 5), (7, 6))
ENDS = ((40, 0, 7), (41, 0, 6))
ARRIVALS = tuple((m, q) for stage in ((2, 8, 1), (4, 3, 7), (5, 6)) for q in range(3) for m in stage)
HALF = BS // 2
ROUND = tuple(range(1, RING))


def kernel(
    factor, target, inverse, cols_in, pairs_in, out,
    left, own, slab, mate, cols, pairs, mate_pairs, part, far, inv_out, inv_in, near, goal,
    local_sem, win_send, win_recv, end_send, mate_send, mate_recv, list_send, list_recv,
    sum_send, sum_recv, inv_send, inv_recv, greet,
):
    group = lax.axis_index("rows")
    slot = lax.axis_index("inner")
    ring_at = slot // 2
    core = slot % 2
    other = slot + 1 - 2 * core
    first_row = group * 2 - BAND
    my_slice = pl.ds(pl.multiple_of(ring_at * SLICE, SLICE), SLICE)

    def along(step):
        return (group + step, slot)

    def around(step):
        return (group, lax.rem(ring_at + step + RING, RING) * 2 + core)

    sibling = (group, other)

    loads = [
        pltpu.make_async_copy(factor.at[:, slot], own.at[0], local_sem.at[0]),
        pltpu.make_async_copy(inverse.at[:, my_slice], slab.at[0], local_sem.at[1]),
        pltpu.make_async_copy(cols_in, cols, local_sem.at[2]),
        pltpu.make_async_copy(pairs_in, pairs, local_sem.at[3]),
        pltpu.make_async_copy(factor.at[:, other], mate.at[0], local_sem.at[4]),
        pltpu.make_async_copy(target, goal, local_sem.at[5]),
        pltpu.make_async_copy(factor, left, local_sem.at[6]),
    ]

    def remote(source, destination, send_sem, recv_sem, device):
        return pltpu.make_async_remote_copy(
            src_ref=source, dst_ref=destination, send_sem=send_sem, recv_sem=recv_sem,
            device_id=device, device_id_type=MESH,
        )

    def active(k, m):
        return jnp.logical_and(group >= k, group - k + max(k, m) < GROUPS)

    steps = {}
    for k, m in WINDOW:
        d = m - k
        sends = active(k, m)
        comes = jnp.logical_and(group >= m, group - m + max(k, m) < GROUPS)
        if d in steps:
            sends = jnp.logical_or(sends, steps[d][0])
            comes = jnp.logical_or(comes, steps[d][1])
        steps[d] = (sends, comes)
    for g, k, m in ENDS:
        d = m - k
        sends, comes = group == g, group == g + d
        if d in steps:
            sends = jnp.logical_or(sends, steps[d][0])
            comes = jnp.logical_or(comes, steps[d][1])
        steps[d] = (sends, comes)

    barrier = pltpu.get_barrier_semaphore()
    for step in (1, -1):
        pl.semaphore_signal(barrier, inc=1, device_id=around(step), device_id_type=MESH)
    pl.semaphore_signal(barrier, inc=1, device_id=sibling, device_id_type=MESH)
    partners = jnp.int32(3)
    for d, (sends, comes) in steps.items():
        @pl.when(comes)
        def _():
            pl.semaphore_signal(barrier, inc=1, device_id=along(-d), device_id_type=MESH)
        partners = partners + sends.astype(jnp.int32)
    for load in loads:
        load.start()
    loads[0].wait()
    loads[1].wait()
    pl.semaphore_wait(barrier, partners)

    def piece(k, q):
        return slab.at[k] if q == 2 else own.at[k, :, pl.ds(q * HALF, HALF)]

    def window_copy(k, m, q, send_sem):
        return remote(piece(k, q), piece(m, q), send_sem, win_recv.at[m - 1, q], along(m - k))

    def mate_copy(k, q):
        place = pl.ds(q * HALF, HALF)
        return remote(
            own.at[k, :, place], mate.at[k, :, place],
            mate_send.at[k - 1, q], mate_recv.at[k - 1, q], sibling,
        )

    def pass_on(held, q):
        for n, (k, m) in enumerate(WINDOW):
            if k == held:
                @pl.when(active(k, m))
                def _():
                    window_copy(k, m, q, win_send.at[n, q]).start()
        for n, (g, k, m) in enumerate(ENDS):
            if k == held:
                @pl.when(group == g)
                def _():
                    window_copy(k, m, q, end_send.at[n, q]).start()
        if held and q < 2:
            mate_copy(held, q).start()

    list_copy = remote(pairs, mate_pairs, list_send.at[0], list_recv.at[0], sibling)

    def greeting(n):
        for way, step in enumerate((1, -1)):
            pl.semaphore_signal(greet.at[n, way], inc=1, device_id=around(step), device_id_type=MESH)

    def greeted(n):
        for way in range(2):
            pl.semaphore_wait(greet.at[n, way], 1)

    for q in range(3):
        pass_on(0, q)
    greeting(0)
    loads[3].wait()
    list_copy.start()

    def arrive(m, q):
        @pl.when(group >= m)
        def _():
            window_copy(0, m, q, win_send.at[0, q]).wait_recv()
            pass_on(m, q)

    def mates(q):
        for m in range(1, HOPS + 1):
            @pl.when(group >= m)
            def _():
                mate_copy(m, q).wait_recv()

    pending = list(ARRIVALS)

    def gather(upto):
        while pending:
            m, q = pending.pop(0)
            arrive(m, q)
            if (m, q) == upto:
                return

    for n in range(3):
        gather(ARRIVALS[3 * n + 2])
        greeted(n)
        if n < 2:
            greeting(n + 1)
    gather(None)
    for load in loads[2:3] + loads[4:]:
        load.wait()
    list_copy.wait_recv()
    for q in range(2):
        mates(q)

    def locate(row, column):
        relative = cols[row, column] - first_row
        back = HOPS - lax.shift_right_arithmetic(relative, 1)
        return jnp.clip(back, 0, HOPS), relative & 1

    def partial_sums(e):
        column = lax.rem(ring_at + e, RING) * 2 + core
        totals = [jnp.zeros((BS, BS), jnp.float32) for _ in range(2)]
        for table, window in ((pairs, own), (mate_pairs, mate)):
            for s in range(2):
                row = table[0, 0, 0, s, column]
                a = table[1, 0, 0, s, column]
                live = table[2, 0, 0, s, column]
                back, half = locate(row, column)
                product = lax.dot_general(
                    left[row, a], window[back, half],
                    (((1,), (1,)), ((), ())), preferred_element_type=jnp.float32,
                )
                for i in range(2):
                    wanted = jnp.logical_and(live == 1, row == i)
                    totals[i] = totals[i] + jnp.where(wanted, product, 0.0)
        return totals

    sent = []

    def hold(e):
        for i, total in enumerate(partial_sums(e)):
            part[e, i] = total.astype(jnp.bfloat16)

    def sum_copy(n):
        source, destination, step = {
            0: (part.at[3], near.at[0], 1),
            1: (part.at[5], near.at[1], -1),
            2: (part.at[4, 0], far.at[0], -2),
            3: (part.at[4, 1], far.at[1], 2),
            4: (part.at[1], near.at[2], 1),
            5: (part.at[7], near.at[3], -1),
            6: (part.at[2], near.at[4], 2),
            7: (part.at[6], near.at[5], -2),
        }[n]
        return remote(source, destination, sum_send.at[n], sum_recv.at[n], around(step))

    def inverse_copy(e, place):
        return remote(inv_out.at[e], inv_in.at[:, place], inv_send.at[e - 1], inv_recv.at[e - 1], around(e))

    def send(copy):
        copy.start()
        sent.append(copy)

    hold(3)
    send(sum_copy(0))
    hold(5)
    send(sum_copy(1))
    hold(4)
    send(sum_copy(2))
    send(sum_copy(3))
    for e in (4, 3, 5, 2, 6, 1, 7, 0):
        column = lax.rem(ring_at + e, RING) * 2 + core
        for i in range(2):
            back, half = locate(i, column)
            inv_out[e, i] = slab[back, half]
        if e:
            send(inverse_copy(e, my_slice))
    hold(1)
    send(sum_copy(4))
    hold(7)
    send(sum_copy(5))
    for e, n, first, second, extra in ((2, 6, 0, 3, 1), (6, 7, 1, 2, 0)):
        totals = partial_sums(e)
        sum_copy(first).wait_recv()
        sum_copy(second).wait_recv()
        for i in range(2):
            total = totals[i] + near[first, i].astype(jnp.float32)
            if i == extra:
                total = total + far[extra].astype(jnp.float32)
            part[e, i] = total.astype(jnp.bfloat16)
        send(sum_copy(n))
    totals = partial_sums(0)
    inv_in[:, my_slice, :] = inv_out[0]
    for n in (4, 5, 6, 7):
        sum_copy(n).wait_recv()
        for i in range(2):
            totals[i] = totals[i] + near[n - 2, i].astype(jnp.float32)
    for e in ROUND:
        start = lax.rem(ring_at - e + RING, RING) * SLICE
        inverse_copy(e, pl.ds(pl.multiple_of(start, SLICE), SLICE)).wait_recv()
    for i in range(2):
        difference = (goal[i, 0].astype(jnp.float32) - totals[i]).astype(jnp.bfloat16)
        result = jnp.dot(difference, inv_in[i], preferred_element_type=jnp.float32)
        result = jnp.where(cols[i, slot] < 0, 0.0, result)
        out[i, 0] = result.astype(jnp.bfloat16)
    for copy in sent:
        copy.wait_send()
    list_copy.wait_send()
    for q in range(3):
        for n, (k, m) in enumerate(WINDOW):
            @pl.when(active(k, m))
            def _():
                window_copy(k, m, q, win_send.at[n, q]).wait_send()
        for n, (g, k, m) in enumerate(ENDS):
            @pl.when(group == g)
            def _():
                window_copy(k, m, q, end_send.at[n, q]).wait_send()
        if q < 2:
            for m in range(1, HOPS + 1):
                @pl.when(group >= m)
                def _():
                    mate_copy(m, q).wait_send()


def per_device(factor, target_blocks, diag_inverse, cols, pair_list):
    bf16 = jnp.bfloat16
    anywhere = pl.BlockSpec(memory_space=pltpu.HBM)
    dma = pltpu.SemaphoreType.DMA
    return pl.pallas_call(
        kernel,
        out_shape=jax.ShapeDtypeStruct((2, 1, BS, BS), bf16),
        in_specs=[anywhere] * 5,
        out_specs=pl.BlockSpec(memory_space=pltpu.VMEM),
        scratch_shapes=[
            pltpu.VMEM((2, 16, BS, BS), bf16),
            pltpu.VMEM((HOPS + 1, 2, BS, BS), bf16),
            pltpu.VMEM((HOPS + 1, 2, SLICE, BS), bf16),
            pltpu.VMEM((HOPS + 1, 2, BS, BS), bf16),
            pltpu.SMEM((2, 16), jnp.int32),
            pltpu.SMEM((3, 1, 1, 2, 16), jnp.int32),
            pltpu.SMEM((3, 1, 1, 2, 16), jnp.int32),
            pltpu.VMEM((RING, 2, BS, BS), bf16),
            pltpu.VMEM((2, BS, BS), bf16),
            pltpu.VMEM((RING, 2, SLICE, BS), bf16),
            pltpu.VMEM((2, BS, BS), bf16),
            pltpu.VMEM((6, 2, BS, BS), bf16),
            pltpu.VMEM((2, 1, BS, BS), bf16),
            dma((7,)),
            dma((len(WINDOW), 3)),
            dma((HOPS, 3)),
            dma((len(ENDS), 3)),
            dma((HOPS, 2)),
            dma((HOPS, 2)),
            dma((1,)),
            dma((1,)),
            dma((8,)),
            dma((8,)),
            dma((RING - 1,)),
            dma((RING - 1,)),
            pltpu.SemaphoreType.REGULAR((3, 2)),
        ],
        compiler_params=pltpu.CompilerParams(
            collective_id=0, has_side_effects=True, vmem_limit_bytes=60 * 1024 * 1024
        ),
        name="sweep",
    )(factor, target_blocks, diag_inverse, cols, jnp.swapaxes(pair_list, 3, 4))


def solution(mesh):
    placed = (
        P("rows", None, None, None),
        P("rows", "inner", None, None),
        P("rows", None, None),
        P("rows", None),
        P(None, "rows", "inner", None, None),
    )
    return jax.shard_map(
        per_device,
        mesh=mesh,
        in_specs=placed,
        out_specs=P("rows", "inner", None, None),
        check_vma=False,
    )
```

```python
import jax
import jax.numpy as jnp
from jax import lax
from jax.experimental import pallas as pl
from jax.experimental.pallas import tpu as pltpu
from jax.sharding import PartitionSpec as P

MESH = pl.DeviceIdType.MESH
BAND = 16
BS = 128
GROUPS = 48
RING = 8
HOPS = 8
SLICE = 16
WINDOW = ((0, 2), (0, 8), (0, 1), (2, 4), (2, 3), (8, 7), (4, 5), (7, 6))
ENDS = ((40, 4, 6), (41, 4, 6), (40, 6, 7))
ARRIVALS = tuple((m, q) for stage in ((2, 8, 1), (4, 3, 7), (5, 6)) for q in range(3) for m in stage)
HALF = BS // 2
KEPT = {0: 0, 2: 1, 6: 2}
ROUND = tuple(range(1, RING))


def kernel(
    factor, target, inverse, cols_in, pairs_in, out,
    left, own_0, own_1, slab, mate_0, mate_1, cols, pairs, mate_pairs, part, far, inv_out, inv_in, near, goal, kept, turned,
    local_sem, win_send, win_recv, end_send, mate_send, mate_recv, list_send, list_recv,
    sum_send, sum_recv, inv_send, inv_recv, greet,
):
    own, mate = (own_0, own_1), (mate_0, mate_1)
    group = lax.axis_index("rows")
    slot = lax.axis_index("inner")
    ring_at = slot // 2
    core = slot % 2
    other = slot + 1 - 2 * core
    first_row = group * 2 - BAND
    my_slice = pl.ds(pl.multiple_of(ring_at * SLICE, SLICE), SLICE)

    def along(step):
        return (group + step, slot)

    def around(step):
        return (group, lax.rem(ring_at + step + RING, RING) * 2 + core)

    sibling = (group, other)

    loads = [
        pltpu.make_async_copy(factor.at[:, slot, pl.ds(0, HALF)], own_0.at[0], local_sem.at[0]),
        pltpu.make_async_copy(factor.at[:, slot, pl.ds(HALF, HALF)], own_1.at[0], local_sem.at[1]),
        pltpu.make_async_copy(inverse.at[:, my_slice], slab.at[0], local_sem.at[2]),
        pltpu.make_async_copy(pairs_in, pairs, local_sem.at[3]),
        pltpu.make_async_copy(cols_in, cols, local_sem.at[4]),
        pltpu.make_async_copy(factor.at[:, other, pl.ds(0, HALF)], mate_0.at[0], local_sem.at[5]),
        pltpu.make_async_copy(factor.at[:, other, pl.ds(HALF, HALF)], mate_1.at[0], local_sem.at[6]),
        pltpu.make_async_copy(target, goal, local_sem.at[7]),
        pltpu.make_async_copy(factor, left, local_sem.at[8]),
    ]

    def remote(source, destination, send_sem, recv_sem, device):
        return pltpu.make_async_remote_copy(
            src_ref=source, dst_ref=destination, send_sem=send_sem, recv_sem=recv_sem,
            device_id=device, device_id_type=MESH,
        )

    def active(k, m):
        reach = 8 if k > m else m
        return jnp.logical_and(group >= k, group - k + reach < GROUPS)

    steps = {}
    for k, m in WINDOW:
        d = m - k
        sends = active(k, m)
        comes = jnp.logical_and(group >= m, group - m + (8 if k > m else m) < GROUPS)
        if d in steps:
            sends = jnp.logical_or(sends, steps[d][0])
            comes = jnp.logical_or(comes, steps[d][1])
        steps[d] = (sends, comes)
    for g, k, m in ENDS:
        d = m - k
        sends, comes = group == g + k, group == g + m
        if d in steps:
            sends = jnp.logical_or(sends, steps[d][0])
            comes = jnp.logical_or(comes, steps[d][1])
        steps[d] = (sends, comes)

    barrier = pltpu.get_barrier_semaphore()
    for step in (1, -1):
        pl.semaphore_signal(barrier, inc=1, device_id=around(step), device_id_type=MESH)
    pl.semaphore_signal(barrier, inc=1, device_id=sibling, device_id_type=MESH)
    partners = jnp.int32(3)
    for d, (sends, comes) in steps.items():
        @pl.when(comes)
        def _():
            pl.semaphore_signal(barrier, inc=1, device_id=along(-d), device_id_type=MESH)
        partners = partners + sends.astype(jnp.int32)
    for load in loads:
        load.start()
    for load in loads[:3]:
        load.wait()
    pl.semaphore_wait(barrier, partners)

    def piece(k, q):
        return slab.at[k] if q == 2 else own[q].at[k]

    def window_copy(k, m, q, send_sem):
        return remote(piece(k, q), piece(m, q), send_sem, win_recv.at[m - 1, q], along(m - k))

    def mate_copy(k, q):
        return remote(own[q].at[k], mate[q].at[k], mate_send.at[k - 1, q], mate_recv.at[k - 1, q], sibling)

    def pass_on(held, q):
        for n, (k, m) in enumerate(WINDOW):
            if k == held:
                @pl.when(active(k, m))
                def _():
                    window_copy(k, m, q, win_send.at[n, q]).start()
        for n, (g, k, m) in enumerate(ENDS):
            if k == held:
                @pl.when(group == g + k)
                def _():
                    window_copy(k, m, q, end_send.at[n, q]).start()
        if held and q < 2:
            mate_copy(held, q).start()

    list_copy = remote(pairs, mate_pairs, list_send.at[0], list_recv.at[0], sibling)

    def greeting(n):
        for way, step in enumerate((1, -1)):
            pl.semaphore_signal(greet.at[n, way], inc=1, device_id=around(step), device_id_type=MESH)

    def greeted(n):
        for way in range(2):
            pl.semaphore_wait(greet.at[n, way], 1)

    for q in range(3):
        pass_on(0, q)
    greeting(0)
    loads[3].wait()
    list_copy.start()

    def arrive(m, q):
        @pl.when(group >= m)
        def _():
            window_copy(0, m, q, win_send.at[0, q]).wait_recv()
            pass_on(m, q)

    def mates(q):
        for m in range(1, HOPS + 1):
            @pl.when(group >= m)
            def _():
                mate_copy(m, q).wait_recv()

    pending = list(ARRIVALS)

    def gather(upto):
        while pending:
            m, q = pending.pop(0)
            arrive(m, q)
            if (m, q) == upto:
                return

    for n in range(3):
        gather(ARRIVALS[3 * n + 2])
        greeted(n)
        if n < 2:
            greeting(n + 1)

    def locate(row, column):
        relative = cols[row, column] - first_row
        back = HOPS - lax.shift_right_arithmetic(relative, 1)
        return jnp.clip(back, 0, HOPS), relative & 1

    def partial_sums(e, q):
        column = lax.rem(ring_at + e, RING) * 2 + core
        totals = [jnp.zeros((HALF, BS), jnp.float32) for _ in range(2)]
        for table, window in ((pairs, own), (mate_pairs, mate)):
            for s in range(2):
                row = table[0, 0, 0, s, column]
                a = table[1, 0, 0, s, column]
                live = table[2, 0, 0, s, column]
                back, half = locate(row, column)
                product = lax.dot_general(
                    window[q][back, half], left[row, a],
                    (((1,), (1,)), ((), ())), preferred_element_type=jnp.float32,
                )
                for i in range(2):
                    wanted = jnp.logical_and(live == 1, row == i)
                    totals[i] = totals[i] + jnp.where(wanted, product, 0.0)
        return totals

    sent = []

    def hold(e, q):
        for i, total in enumerate(partial_sums(e, q)):
            part[q, e, i] = total.astype(jnp.bfloat16)

    def keep(e, q):
        for i, total in enumerate(partial_sums(e, q)):
            kept[q, KEPT[e], i] = total

    def sum_copy(n, q):
        source, destination, step = {
            0: (part.at[q, 3], near.at[q, 0], 1),
            1: (part.at[q, 5], near.at[q, 1], -1),
            2: (part.at[q, 4, 0], far.at[q, 0], -2),
            3: (part.at[q, 4, 1], far.at[q, 1], 2),
            4: (part.at[q, 1], near.at[q, 2], 1),
            5: (part.at[q, 7], near.at[q, 3], -1),
            6: (part.at[q, 2], near.at[q, 4], 2),
            7: (part.at[q, 6], near.at[q, 5], -2),
        }[n]
        return remote(source, destination, sum_send.at[n, q], sum_recv.at[n, q], around(step))

    def inverse_copy(e, place):
        return remote(inv_out.at[e], inv_in.at[:, place], inv_send.at[e - 1], inv_recv.at[e - 1], around(e))

    def send(copy):
        copy.start()
        sent.append(copy)

    def first_sums(q):
        hold(4, q)
        send(sum_copy(2, q))
        send(sum_copy(3, q))
        hold(3, q)
        send(sum_copy(0, q))
        hold(5, q)
        send(sum_copy(1, q))
        hold(1, q)
        send(sum_copy(4, q))
        hold(7, q)
        send(sum_copy(5, q))
        for e in (2, 6, 0):
            keep(e, q)

    def second_sums(q):
        for e, n, first, second, extra in ((2, 6, 0, 3, 1), (6, 7, 1, 2, 0)):
            sum_copy(first, q).wait_recv()
            sum_copy(second, q).wait_recv()
            for i in range(2):
                total = kept[q, KEPT[e], i] + near[q, first, i].astype(jnp.float32)
                if i == extra:
                    total = total + far[q, extra].astype(jnp.float32)
                part[q, e, i] = total.astype(jnp.bfloat16)
            send(sum_copy(n, q))

    def last_sums(q):
        totals = [kept[q, 0, i] for i in range(2)]
        for n in (4, 5, 6, 7):
            sum_copy(n, q).wait_recv()
            for i in range(2):
                totals[i] = totals[i] + near[q, n - 2, i].astype(jnp.float32)
        results = []
        for i in range(2):
            rows = pl.ds(q * HALF, HALF)
            difference = (turned[i, rows] - totals[i]).astype(jnp.bfloat16)
            results.append(lax.dot_general(
                difference, inv_in[i, rows], (((0,), (0,)), ((), ())), preferred_element_type=jnp.float32
            ))
        return results

    gather((6, 0))
    for load in loads[4:]:
        load.wait()
    list_copy.wait_recv()
    for i in range(2):
        turned[i] = goal[i, 0].astype(jnp.float32).T
    mates(0)
    first_sums(0)
    gather((6, 1))
    mates(1)
    first_sums(1)
    gather(None)
    for e in (4, 3, 5, 2, 6, 1, 7, 0):
        column = lax.rem(ring_at + e, RING) * 2 + core
        for i in range(2):
            back, half = locate(i, column)
            inv_out[e, i] = slab[back, half]
        if e:
            send(inverse_copy(e, my_slice))
    inv_in[:, my_slice, :] = inv_out[0]
    for q in range(2):
        second_sums(q)
    for e in ROUND:
        start = lax.rem(ring_at - e + RING, RING) * SLICE
        inverse_copy(e, pl.ds(pl.multiple_of(start, SLICE), SLICE)).wait_recv()
    lower = last_sums(0)
    upper = last_sums(1)
    for i in range(2):
        result = jnp.where(cols[i, slot] < 0, 0.0, lower[i] + upper[i])
        out[i, 0] = result.astype(jnp.bfloat16)
    for copy in sent:
        copy.wait_send()
    list_copy.wait_send()
    for q in range(3):
        for n, (k, m) in enumerate(WINDOW):
            @pl.when(active(k, m))
            def _():
                window_copy(k, m, q, win_send.at[n, q]).wait_send()
        for n, (g, k, m) in enumerate(ENDS):
            @pl.when(group == g + k)
            def _():
                window_copy(k, m, q, end_send.at[n, q]).wait_send()
        if q < 2:
            for m in range(1, HOPS + 1):
                @pl.when(group >= m)
                def _():
                    mate_copy(m, q).wait_send()


def per_device(factor, target_blocks, diag_inverse, cols, pair_list):
    bf16 = jnp.bfloat16
    anywhere = pl.BlockSpec(memory_space=pltpu.HBM)
    dma = pltpu.SemaphoreType.DMA
    return pl.pallas_call(
        kernel,
        out_shape=jax.ShapeDtypeStruct((2, 1, BS, BS), bf16),
        in_specs=[anywhere] * 5,
        out_specs=pl.BlockSpec(memory_space=pltpu.VMEM),
        scratch_shapes=[
            pltpu.VMEM((2, 16, BS, BS), bf16),
            pltpu.VMEM((HOPS + 1, 2, HALF, BS), bf16),
            pltpu.VMEM((HOPS + 1, 2, HALF, BS), bf16),
            pltpu.VMEM((HOPS + 1, 2, SLICE, BS), bf16),
            pltpu.VMEM((HOPS + 1, 2, HALF, BS), bf16),
            pltpu.VMEM((HOPS + 1, 2, HALF, BS), bf16),
            pltpu.SMEM((2, 16), jnp.int32),
            pltpu.SMEM((3, 1, 1, 2, 16), jnp.int32),
            pltpu.SMEM((3, 1, 1, 2, 16), jnp.int32),
            pltpu.VMEM((2, RING, 2, HALF, BS), bf16),
            pltpu.VMEM((2, 2, HALF, BS), bf16),
            pltpu.VMEM((RING, 2, SLICE, BS), bf16),
            pltpu.VMEM((2, BS, BS), bf16),
            pltpu.VMEM((2, 6, 2, HALF, BS), bf16),
            pltpu.VMEM((2, 1, BS, BS), bf16),
            pltpu.VMEM((2, 3, 2, HALF, BS), jnp.float32),
            pltpu.VMEM((2, BS, BS), jnp.float32),
            dma((9,)),
            dma((len(WINDOW), 3)),
            dma((HOPS, 3)),
            dma((len(ENDS), 3)),
            dma((HOPS, 2)),
            dma((HOPS, 2)),
            dma((1,)),
            dma((1,)),
            dma((8, 2)),
            dma((8, 2)),
            dma((RING - 1,)),
            dma((RING - 1,)),
            pltpu.SemaphoreType.REGULAR((3, 2)),
        ],
        compiler_params=pltpu.CompilerParams(
            collective_id=0, has_side_effects=True, vmem_limit_bytes=60 * 1024 * 1024
        ),
        name="sweep",
    )(factor, target_blocks, diag_inverse, cols, jnp.swapaxes(pair_list, 3, 4))


def solution(mesh):
    placed = (
        P("rows", None, None, None),
        P("rows", "inner", None, None),
        P("rows", None, None),
        P("rows", None),
        P(None, "rows", "inner", None, None),
    )
    return jax.shard_map(
        per_device,
        mesh=mesh,
        in_specs=placed,
        out_specs=P("rows", "inner", None, None),
        check_vma=False,
    )
```

```python
import jax
import jax.numpy as jnp
from jax import lax
from jax.experimental import pallas as pl
from jax.experimental.pallas import tpu as pltpu
from jax.sharding import PartitionSpec as P

MESH = pl.DeviceIdType.MESH
BAND = 16
BS = 128
GROUPS = 48
RING = 8
HOPS = 8
SLICE = 16
WINDOW = ((0, 2), (0, 8), (2, 5), (2, 4), (2, 3), (2, 1), (8, 6), (8, 7))
ENDS = ((40, 5, 7), (40, 5, 6), (41, 5, 6), (46, 0, 1))
ARRIVALS = tuple((m, q) for stage in ((2, 8), (1, 3, 7, 4, 5, 6)) for q in range(3) for m in stage)
HALF = BS // 2
KEPT = {0: 0, 2: 1, 6: 2}
ROUND = tuple(range(1, RING))


def kernel(
    factor, target, inverse, cols_in, pairs_in, out,
    left, own_0, own_1, slab, mate_0, mate_1, cols, pairs, mate_pairs, part, far, inv_out, inv_in, near, goal, kept, turned,
    local_sem, win_send, win_recv, end_send, mate_send, mate_recv, list_send, list_recv,
    sum_send, sum_recv, inv_send, inv_recv, greet,
):
    own, mate = (own_0, own_1), (mate_0, mate_1)
    group = lax.axis_index("rows")
    slot = lax.axis_index("inner")
    ring_at = slot // 2
    core = slot % 2
    other = slot + 1 - 2 * core
    first_row = group * 2 - BAND
    my_slice = pl.ds(pl.multiple_of(ring_at * SLICE, SLICE), SLICE)

    def along(step):
        return (group + step, slot)

    def around(step):
        return (group, lax.rem(ring_at + step + RING, RING) * 2 + core)

    sibling = (group, other)

    loads = [
        pltpu.make_async_copy(factor.at[:, slot, pl.ds(0, HALF)], own_0.at[0], local_sem.at[0]),
        pltpu.make_async_copy(factor.at[:, slot, pl.ds(HALF, HALF)], own_1.at[0], local_sem.at[1]),
        pltpu.make_async_copy(inverse.at[:, my_slice], slab.at[0], local_sem.at[2]),
        pltpu.make_async_copy(pairs_in, pairs, local_sem.at[3]),
        pltpu.make_async_copy(cols_in, cols, local_sem.at[4]),
        pltpu.make_async_copy(factor.at[:, other, pl.ds(0, HALF)], mate_0.at[0], local_sem.at[5]),
        pltpu.make_async_copy(factor.at[:, other, pl.ds(HALF, HALF)], mate_1.at[0], local_sem.at[6]),
        pltpu.make_async_copy(target, goal, local_sem.at[7]),
        pltpu.make_async_copy(factor, left, local_sem.at[8]),
    ]

    def remote(source, destination, send_sem, recv_sem, device):
        return pltpu.make_async_remote_copy(
            src_ref=source, dst_ref=destination, send_sem=send_sem, recv_sem=recv_sem,
            device_id=device, device_id_type=MESH,
        )

    def active(k, m):
        return jnp.logical_and(group >= k, group - k + max(k, m) < GROUPS)

    steps = {}
    for k, m in WINDOW:
        d = m - k
        sends = active(k, m)
        comes = jnp.logical_and(group >= m, group - m + max(k, m) < GROUPS)
        if d in steps:
            sends = jnp.logical_or(sends, steps[d][0])
            comes = jnp.logical_or(comes, steps[d][1])
        steps[d] = (sends, comes)
    for g, k, m in ENDS:
        d = m - k
        sends, comes = group == g + k, group == g + m
        if d in steps:
            sends = jnp.logical_or(sends, steps[d][0])
            comes = jnp.logical_or(comes, steps[d][1])
        steps[d] = (sends, comes)

    barrier = pltpu.get_barrier_semaphore()
    for step in (1, -1):
        pl.semaphore_signal(barrier, inc=1, device_id=around(step), device_id_type=MESH)
    pl.semaphore_signal(barrier, inc=1, device_id=sibling, device_id_type=MESH)
    partners = jnp.int32(3)
    for d, (sends, comes) in steps.items():
        @pl.when(comes)
        def _():
            pl.semaphore_signal(barrier, inc=1, device_id=along(-d), device_id_type=MESH)
        partners = partners + sends.astype(jnp.int32)
    for load in loads:
        load.start()
    for load in loads[:3]:
        load.wait()
    pl.semaphore_wait(barrier, partners)

    def piece(k, q):
        return slab.at[k] if q == 2 else own[q].at[k]

    def window_copy(k, m, q, send_sem):
        return remote(piece(k, q), piece(m, q), send_sem, win_recv.at[m - 1, q], along(m - k))

    def mate_copy(k, q):
        return remote(own[q].at[k], mate[q].at[k], mate_send.at[k - 1, q], mate_recv.at[k - 1, q], sibling)

    def pass_on(held, q):
        for n, (k, m) in enumerate(WINDOW):
            if k == held:
                @pl.when(active(k, m))
                def _():
                    window_copy(k, m, q, win_send.at[n, q]).start()
        for n, (g, k, m) in enumerate(ENDS):
            if k == held:
                @pl.when(group == g + k)
                def _():
                    window_copy(k, m, q, end_send.at[n, q]).start()
        if held and q < 2:
            mate_copy(held, q).start()

    list_copy = remote(pairs, mate_pairs, list_send.at[0], list_recv.at[0], sibling)

    def greeting(n):
        for way, step in enumerate((1, -1)):
            pl.semaphore_signal(greet.at[n, way], inc=1, device_id=around(step), device_id_type=MESH)

    def greeted(n):
        for way in range(2):
            pl.semaphore_wait(greet.at[n, way], 1)

    for q in range(3):
        pass_on(0, q)
    greeting(0)
    loads[3].wait()
    list_copy.start()

    def arrive(m, q):
        @pl.when(group >= m)
        def _():
            window_copy(0, m, q, win_send.at[0, q]).wait_recv()
            pass_on(m, q)

    def mates(q):
        for m in range(1, HOPS + 1):
            @pl.when(group >= m)
            def _():
                mate_copy(m, q).wait_recv()

    pending = list(ARRIVALS)

    def gather(upto):
        while pending:
            m, q = pending.pop(0)
            arrive(m, q)
            if (m, q) == upto:
                return

    for n in range(3):
        gather(ARRIVALS[3 * n + 2])
        greeted(n)
        if n < 2:
            greeting(n + 1)

    def locate(row, column):
        relative = cols[row, column] - first_row
        back = HOPS - lax.shift_right_arithmetic(relative, 1)
        return jnp.clip(back, 0, HOPS), relative & 1

    def partial_sums(e, q):
        column = lax.rem(ring_at + e, RING) * 2 + core
        totals = [jnp.zeros((HALF, BS), jnp.float32) for _ in range(2)]
        for table, window in ((pairs, own), (mate_pairs, mate)):
            for s in range(2):
                row = table[0, 0, 0, s, column]
                a = table[1, 0, 0, s, column]
                live = table[2, 0, 0, s, column]
                back, half = locate(row, column)
                product = lax.dot_general(
                    window[q][back, half], left[row, a],
                    (((1,), (1,)), ((), ())), preferred_element_type=jnp.float32,
                )
                for i in range(2):
                    wanted = jnp.logical_and(live == 1, row == i)
                    totals[i] = totals[i] + jnp.where(wanted, product, 0.0)
        return totals

    sent = []

    def hold(e, q):
        for i, total in enumerate(partial_sums(e, q)):
            part[q, e, i] = total.astype(jnp.bfloat16)

    def keep(e, q):
        for i, total in enumerate(partial_sums(e, q)):
            kept[q, KEPT[e], i] = total

    def sum_copy(n, q):
        source, destination, step = {
            0: (part.at[q, 3], near.at[q, 0], 1),
            1: (part.at[q, 5], near.at[q, 1], -1),
            2: (part.at[q, 4, 0], far.at[q, 0], -2),
            3: (part.at[q, 4, 1], far.at[q, 1], 2),
            4: (part.at[q, 1], near.at[q, 2], 1),
            5: (part.at[q, 7], near.at[q, 3], -1),
            6: (part.at[q, 2], near.at[q, 4], 2),
            7: (part.at[q, 6], near.at[q, 5], -2),
        }[n]
        return remote(source, destination, sum_send.at[n, q], sum_recv.at[n, q], around(step))

    def inverse_copy(e, place):
        return remote(inv_out.at[e], inv_in.at[:, place], inv_send.at[e - 1], inv_recv.at[e - 1], around(e))

    def send(copy):
        copy.start()
        sent.append(copy)

    def first_sums(q):
        hold(4, q)
        send(sum_copy(2, q))
        send(sum_copy(3, q))
        hold(3, q)
        send(sum_copy(0, q))
        hold(5, q)
        send(sum_copy(1, q))
        hold(1, q)
        send(sum_copy(4, q))
        hold(7, q)
        send(sum_copy(5, q))
        for e in (2, 6, 0):
            keep(e, q)

    def second_sums(q):
        for e, n, first, second, extra in ((2, 6, 0, 3, 1), (6, 7, 1, 2, 0)):
            sum_copy(first, q).wait_recv()
            sum_copy(second, q).wait_recv()
            for i in range(2):
                total = kept[q, KEPT[e], i] + near[q, first, i].astype(jnp.float32)
                if i == extra:
                    total = total + far[q, extra].astype(jnp.float32)
                part[q, e, i] = total.astype(jnp.bfloat16)
            send(sum_copy(n, q))

    def last_sums(q):
        totals = [kept[q, 0, i] for i in range(2)]
        for n in (4, 5, 6, 7):
            sum_copy(n, q).wait_recv()
            for i in range(2):
                totals[i] = totals[i] + near[q, n - 2, i].astype(jnp.float32)
        results = []
        for i in range(2):
            rows = pl.ds(q * HALF, HALF)
            difference = (turned[i, rows] - totals[i]).astype(jnp.bfloat16)
            results.append(lax.dot_general(
                difference, inv_in[i, rows], (((0,), (0,)), ((), ())), preferred_element_type=jnp.float32
            ))
        return results

    gather((6, 0))
    for load in loads[4:]:
        load.wait()
    list_copy.wait_recv()
    for i in range(2):
        turned[i] = goal[i, 0].astype(jnp.float32).T
    mates(0)
    first_sums(0)
    gather((6, 1))
    mates(1)
    first_sums(1)
    gather(None)
    second_sums(0)
    for e in (4, 3, 5, 0):
        column = lax.rem(ring_at + e, RING) * 2 + core
        for i in range(2):
            back, half = locate(i, column)
            inv_out[e, i] = slab[back, half]
        if e:
            send(inverse_copy(e, my_slice))
    inv_in[:, my_slice, :] = inv_out[0]
    list_copy.wait_send()
    for q in range(3):
        for n, (k, m) in enumerate(WINDOW):
            @pl.when(active(k, m))
            def _():
                window_copy(k, m, q, win_send.at[n, q]).wait_send()
        for n, (g, k, m) in enumerate(ENDS):
            @pl.when(group == g + k)
            def _():
                window_copy(k, m, q, end_send.at[n, q]).wait_send()
        if q < 2:
            for m in range(1, HOPS + 1):
                @pl.when(group >= m)
                def _():
                    mate_copy(m, q).wait_send()
    second_sums(1)
    for e in (2, 6, 1, 7):
        column = lax.rem(ring_at + e, RING) * 2 + core
        for i in range(2):
            back, half = locate(i, column)
            inv_out[e, i] = slab[back, half]
        if e:
            send(inverse_copy(e, my_slice))
    for e in ROUND:
        start = lax.rem(ring_at - e + RING, RING) * SLICE
        inverse_copy(e, pl.ds(pl.multiple_of(start, SLICE), SLICE)).wait_recv()
    last = sent[-6:]
    for copy in sent[:-6]:
        copy.wait_send()
    lower = last_sums(0)
    upper = last_sums(1)
    for i in range(2):
        result = jnp.where(cols[i, slot] < 0, 0.0, lower[i] + upper[i])
        out[i, 0] = result.astype(jnp.bfloat16)

    for copy in last:
        copy.wait_send()


def per_device(factor, target_blocks, diag_inverse, cols, pair_list):
    bf16 = jnp.bfloat16
    anywhere = pl.BlockSpec(memory_space=pltpu.HBM)
    dma = pltpu.SemaphoreType.DMA
    return pl.pallas_call(
        kernel,
        out_shape=jax.ShapeDtypeStruct((2, 1, BS, BS), bf16),
        in_specs=[anywhere] * 5,
        out_specs=pl.BlockSpec(memory_space=pltpu.VMEM),
        scratch_shapes=[
            pltpu.VMEM((2, 16, BS, BS), bf16),
            pltpu.VMEM((HOPS + 1, 2, HALF, BS), bf16),
            pltpu.VMEM((HOPS + 1, 2, HALF, BS), bf16),
            pltpu.VMEM((HOPS + 1, 2, SLICE, BS), bf16),
            pltpu.VMEM((HOPS + 1, 2, HALF, BS), bf16),
            pltpu.VMEM((HOPS + 1, 2, HALF, BS), bf16),
            pltpu.SMEM((2, 16), jnp.int32),
            pltpu.SMEM((3, 1, 1, 2, 16), jnp.int32),
            pltpu.SMEM((3, 1, 1, 2, 16), jnp.int32),
            pltpu.VMEM((2, RING, 2, HALF, BS), bf16),
            pltpu.VMEM((2, 2, HALF, BS), bf16),
            pltpu.VMEM((RING, 2, SLICE, BS), bf16),
            pltpu.VMEM((2, BS, BS), bf16),
            pltpu.VMEM((2, 6, 2, HALF, BS), bf16),
            pltpu.VMEM((2, 1, BS, BS), bf16),
            pltpu.VMEM((2, 3, 2, HALF, BS), jnp.float32),
            pltpu.VMEM((2, BS, BS), jnp.float32),
            dma((9,)),
            dma((len(WINDOW), 3)),
            dma((HOPS, 3)),
            dma((len(ENDS), 3)),
            dma((HOPS, 2)),
            dma((HOPS, 2)),
            dma((1,)),
            dma((1,)),
            dma((8, 2)),
            dma((8, 2)),
            dma((RING - 1,)),
            dma((RING - 1,)),
            pltpu.SemaphoreType.REGULAR((3, 2)),
        ],
        compiler_params=pltpu.CompilerParams(
            collective_id=0, has_side_effects=True, vmem_limit_bytes=60 * 1024 * 1024
        ),
        name="sweep",
    )(factor, target_blocks, diag_inverse, cols, jnp.swapaxes(pair_list, 3, 4))


def solution(mesh):
    placed = (
        P("rows", None, None, None),
        P("rows", "inner", None, None),
        P("rows", None, None),
        P("rows", None),
        P(None, "rows", "inner", None, None),
    )
    return jax.shard_map(
        per_device,
        mesh=mesh,
        in_specs=placed,
        out_specs=P("rows", "inner", None, None),
        check_vma=False,
    )
```

```python
import jax
import jax.numpy as jnp
from jax import lax
from jax.experimental import pallas as pl
from jax.experimental.pallas import tpu as pltpu
from jax.sharding import PartitionSpec as P

MESH = pl.DeviceIdType.MESH
BAND = 16
BS = 128
GROUPS = 48
RING = 8
HOPS = 8
SLICE = 16
WINDOW = ((0, 2), (0, 8), (2, 5), (2, 4), (2, 3), (2, 1), (8, 6), (8, 7))
ENDS = ((40, 5, 7), (40, 5, 6), (41, 5, 6), (46, 0, 1))
ARRIVALS = tuple((m, q) for stage in ((2, 8), (1, 3, 7, 4, 5, 6)) for q in range(3) for m in stage)
HALF = BS // 2
KEPT = {0: 0, 2: 1, 6: 2}
ROUND = tuple(range(1, RING))


def kernel(
    factor, target, inverse, cols_in, pairs_in, out,
    left, own_0, own_1, slab, mate_0, mate_1, cols, pairs, mate_pairs, part, far, inv_out, inv_in, near, goal, kept, turned,
    local_sem, win_send, win_recv, end_send, mate_send, mate_recv, list_send, list_recv,
    sum_send, sum_recv, inv_send, inv_recv, greet,
):
    own, mate = (own_0, own_1), (mate_0, mate_1)
    group = lax.axis_index("rows")
    slot = lax.axis_index("inner")
    ring_at = slot // 2
    core = slot % 2
    other = slot + 1 - 2 * core
    first_row = group * 2 - BAND
    my_slice = pl.ds(pl.multiple_of(ring_at * SLICE, SLICE), SLICE)

    def along(step):
        return (lax.rem(group + step + GROUPS, GROUPS), slot)

    def around(step):
        return (group, lax.rem(ring_at + step + RING, RING) * 2 + core)

    sibling = (group, other)

    loads = [
        pltpu.make_async_copy(factor.at[:, slot, pl.ds(0, HALF)], own_0.at[0], local_sem.at[0]),
        pltpu.make_async_copy(factor.at[:, slot, pl.ds(HALF, HALF)], own_1.at[0], local_sem.at[1]),
        pltpu.make_async_copy(inverse.at[:, my_slice], slab.at[0], local_sem.at[2]),
        pltpu.make_async_copy(pairs_in, pairs, local_sem.at[3]),
        pltpu.make_async_copy(cols_in, cols, local_sem.at[4]),
        pltpu.make_async_copy(factor.at[:, other, pl.ds(0, HALF)], mate_0.at[0], local_sem.at[5]),
        pltpu.make_async_copy(factor.at[:, other, pl.ds(HALF, HALF)], mate_1.at[0], local_sem.at[6]),
        pltpu.make_async_copy(target, goal, local_sem.at[7]),
        pltpu.make_async_copy(factor, left, local_sem.at[8]),
    ]

    def remote(source, destination, send_sem, recv_sem, device):
        return pltpu.make_async_remote_copy(
            src_ref=source, dst_ref=destination, send_sem=send_sem, recv_sem=recv_sem,
            device_id=device, device_id_type=MESH,
        )

    def active(k, m):
        return jnp.logical_and(group >= k, group - k + max(k, m) < GROUPS)

    steps = {}
    for k, m in WINDOW:
        d = m - k
        sends = active(k, m)
        comes = jnp.logical_and(group >= m, group - m + max(k, m) < GROUPS)
        if d in steps:
            sends = jnp.logical_or(sends, steps[d][0])
            comes = jnp.logical_or(comes, steps[d][1])
        steps[d] = (sends, comes)
    for g, k, m in ENDS:
        d = m - k
        sends, comes = group == g + k, group == g + m
        if d in steps:
            sends = jnp.logical_or(sends, steps[d][0])
            comes = jnp.logical_or(comes, steps[d][1])
        steps[d] = (sends, comes)

    barrier = pltpu.get_barrier_semaphore()
    for step in (1, -1):
        pl.semaphore_signal(barrier, inc=1, device_id=around(step), device_id_type=MESH)
    pl.semaphore_signal(barrier, inc=1, device_id=sibling, device_id_type=MESH)
    partners = jnp.int32(3)
    for d, (sends, comes) in steps.items():
        @pl.when(comes)
        def _():
            pl.semaphore_signal(barrier, inc=1, device_id=along(-d), device_id_type=MESH)
        partners = partners + sends.astype(jnp.int32)
    for load in loads:
        load.start()
    for load in loads[:3]:
        load.wait()
    pl.semaphore_wait(barrier, partners)

    def piece(k, q):
        return slab.at[k] if q == 2 else own[q].at[k]

    def window_copy(k, m, q, send_sem):
        return remote(piece(k, q), piece(m, q), send_sem, win_recv.at[m - 1, q], along(m - k))

    def mate_copy(k, q):
        return remote(own[q].at[k], mate[q].at[k], mate_send.at[k - 1, q], mate_recv.at[k - 1, q], sibling)

    def pass_on(held, q):
        for n, (k, m) in enumerate(WINDOW):
            if k == held:
                @pl.when(active(k, m))
                def _():
                    window_copy(k, m, q, win_send.at[n, q]).start()
        for n, (g, k, m) in enumerate(ENDS):
            if k == held:
                @pl.when(group == g + k)
                def _():
                    window_copy(k, m, q, end_send.at[n, q]).start()
        if held and q < 2:
            mate_copy(held, q).start()

    list_copy = remote(pairs, mate_pairs, list_send.at[0], list_recv.at[0], sibling)

    def greeting(n):
        for way, step in enumerate((1, -1)):
            pl.semaphore_signal(greet.at[n, way], inc=1, device_id=around(step), device_id_type=MESH)

    def greeted(n):
        for way in range(2):
            pl.semaphore_wait(greet.at[n, way], 1)

    for q in range(3):
        pass_on(0, q)
    greeting(0)
    loads[3].wait()
    list_copy.start()

    def arrive(m, q):
        @pl.when(group >= m)
        def _():
            window_copy(0, m, q, win_send.at[0, q]).wait_recv()
            pass_on(m, q)

    def mates(q):
        for m in range(1, HOPS + 1):
            @pl.when(group >= m)
            def _():
                mate_copy(m, q).wait_recv()

    pending = list(ARRIVALS)

    def gather(upto):
        while pending:
            m, q = pending.pop(0)
            arrive(m, q)
            if (m, q) == upto:
                return

    for n in range(3):
        gather(ARRIVALS[3 * n + 2])
        greeted(n)
        if n < 2:
            greeting(n + 1)

    def locate(row, column):
        relative = cols[row, column] - first_row
        back = HOPS - lax.shift_right_arithmetic(relative, 1)
        return jnp.clip(back, 0, HOPS), relative & 1

    def partial_sums(e, q):
        column = lax.rem(ring_at + e, RING) * 2 + core
        totals = [jnp.zeros((HALF, BS), jnp.float32) for _ in range(2)]
        for table, window in ((pairs, own), (mate_pairs, mate)):
            for s in range(2):
                row = table[0, 0, 0, s, column]
                a = table[1, 0, 0, s, column]
                live = table[2, 0, 0, s, column]
                back, half = locate(row, column)
                product = lax.dot_general(
                    window[q][back, half], left[row, a],
                    (((1,), (1,)), ((), ())), preferred_element_type=jnp.float32,
                )
                for i in range(2):
                    wanted = jnp.logical_and(live == 1, row == i)
                    totals[i] = totals[i] + jnp.where(wanted, product, 0.0)
        return totals

    sent = []

    def hold(e, q):
        for i, total in enumerate(partial_sums(e, q)):
            part[q, e, i] = total.astype(jnp.bfloat16)

    def keep(e, q):
        for i, total in enumerate(partial_sums(e, q)):
            kept[q, KEPT[e], i] = total

    def sum_copy(n, q):
        source, destination, step = {
            0: (part.at[q, 3], near.at[q, 0], 1),
            1: (part.at[q, 5], near.at[q, 1], -1),
            2: (part.at[q, 4, 0], far.at[q, 0], -2),
            3: (part.at[q, 4, 1], far.at[q, 1], 2),
            4: (part.at[q, 1], near.at[q, 2], 1),
            5: (part.at[q, 7], near.at[q, 3], -1),
            6: (part.at[q, 2], near.at[q, 4], 2),
            7: (part.at[q, 6], near.at[q, 5], -2),
        }[n]
        return remote(source, destination, sum_send.at[n, q], sum_recv.at[n, q], around(step))

    def inverse_copy(e, place):
        return remote(inv_out.at[e], inv_in.at[:, place], inv_send.at[e - 1], inv_recv.at[e - 1], around(e))

    def send(copy):
        copy.start()
        sent.append(copy)

    def first_sums(q):
        hold(4, q)
        send(sum_copy(2, q))
        send(sum_copy(3, q))
        hold(3, q)
        send(sum_copy(0, q))
        hold(5, q)
        send(sum_copy(1, q))
        hold(1, q)
        send(sum_copy(4, q))
        hold(7, q)
        send(sum_copy(5, q))
        for e in (2, 6, 0):
            keep(e, q)

    def second_sums(q):
        for e, n, first, second, extra in ((2, 6, 0, 3, 1), (6, 7, 1, 2, 0)):
            sum_copy(first, q).wait_recv()
            sum_copy(second, q).wait_recv()
            for i in range(2):
                total = kept[q, KEPT[e], i] + near[q, first, i].astype(jnp.float32)
                if i == extra:
                    total = total + far[q, extra].astype(jnp.float32)
                part[q, e, i] = total.astype(jnp.bfloat16)
            send(sum_copy(n, q))

    def last_sums(q):
        totals = [kept[q, 0, i] for i in range(2)]
        for n in (4, 5, 6, 7):
            sum_copy(n, q).wait_recv()
            for i in range(2):
                totals[i] = totals[i] + near[q, n - 2, i].astype(jnp.float32)
        results = []
        for i in range(2):
            rows = pl.ds(q * HALF, HALF)
            difference = (turned[i, rows] - totals[i]).astype(jnp.bfloat16)
            results.append(lax.dot_general(
                difference, inv_in[i, rows], (((0,), (0,)), ((), ())), preferred_element_type=jnp.float32
            ))
        return results

    gather((6, 0))
    for load in loads[4:]:
        load.wait()
    list_copy.wait_recv()
    for i in range(2):
        turned[i] = goal[i, 0].astype(jnp.float32).T
    mates(0)
    first_sums(0)
    gather((6, 1))
    mates(1)
    first_sums(1)
    gather(None)
    second_sums(0)
    for e in (4, 3, 5, 0):
        column = lax.rem(ring_at + e, RING) * 2 + core
        for i in range(2):
            back, half = locate(i, column)
            inv_out[e, i] = slab[back, half]
        if e:
            send(inverse_copy(e, my_slice))
    inv_in[:, my_slice, :] = inv_out[0]
    list_copy.wait_send()
    for q in range(3):
        for n, (k, m) in enumerate(WINDOW):
            @pl.when(active(k, m))
            def _():
                window_copy(k, m, q, win_send.at[n, q]).wait_send()
        for n, (g, k, m) in enumerate(ENDS):
            @pl.when(group == g + k)
            def _():
                window_copy(k, m, q, end_send.at[n, q]).wait_send()
        if q < 2:
            for m in range(1, HOPS + 1):
                @pl.when(group >= m)
                def _():
                    mate_copy(m, q).wait_send()
    second_sums(1)
    for e in (2, 6, 1, 7):
        column = lax.rem(ring_at + e, RING) * 2 + core
        for i in range(2):
            back, half = locate(i, column)
            inv_out[e, i] = slab[back, half]
        if e:
            send(inverse_copy(e, my_slice))
    for e in ROUND:
        start = lax.rem(ring_at - e + RING, RING) * SLICE
        inverse_copy(e, pl.ds(pl.multiple_of(start, SLICE), SLICE)).wait_recv()
    last = sent[-6:]
    for copy in sent[:-6]:
        copy.wait_send()
    lower = last_sums(0)
    upper = last_sums(1)
    for i in range(2):
        result = jnp.where(cols[i, slot] < 0, 0.0, lower[i] + upper[i])
        out[i, 0] = result.astype(jnp.bfloat16)

    for copy in last:
        copy.wait_send()


def per_device(factor, target_blocks, diag_inverse, cols, pair_list):
    bf16 = jnp.bfloat16
    anywhere = pl.BlockSpec(memory_space=pltpu.HBM)
    dma = pltpu.SemaphoreType.DMA
    return pl.pallas_call(
        kernel,
        out_shape=jax.ShapeDtypeStruct((2, 1, BS, BS), bf16),
        in_specs=[anywhere] * 5,
        out_specs=pl.BlockSpec(memory_space=pltpu.VMEM),
        scratch_shapes=[
            pltpu.VMEM((2, 16, BS, BS), bf16),
            pltpu.VMEM((HOPS + 1, 2, HALF, BS), bf16),
            pltpu.VMEM((HOPS + 1, 2, HALF, BS), bf16),
            pltpu.VMEM((HOPS + 1, 2, SLICE, BS), bf16),
            pltpu.VMEM((HOPS + 1, 2, HALF, BS), bf16),
            pltpu.VMEM((HOPS + 1, 2, HALF, BS), bf16),
            pltpu.SMEM((2, 16), jnp.int32),
            pltpu.SMEM((3, 1, 1, 2, 16), jnp.int32),
            pltpu.SMEM((3, 1, 1, 2, 16), jnp.int32),
            pltpu.VMEM((2, RING, 2, HALF, BS), bf16),
            pltpu.VMEM((2, 2, HALF, BS), bf16),
            pltpu.VMEM((RING, 2, SLICE, BS), bf16),
            pltpu.VMEM((2, BS, BS), bf16),
            pltpu.VMEM((2, 6, 2, HALF, BS), bf16),
            pltpu.VMEM((2, 1, BS, BS), bf16),
            pltpu.VMEM((2, 3, 2, HALF, BS), jnp.float32),
            pltpu.VMEM((2, BS, BS), jnp.float32),
            dma((9,)),
            dma((len(WINDOW), 3)),
            dma((HOPS, 3)),
            dma((len(ENDS), 3)),
            dma((HOPS, 2)),
            dma((HOPS, 2)),
            dma((1,)),
            dma((1,)),
            dma((8, 2)),
            dma((8, 2)),
            dma((RING - 1,)),
            dma((RING - 1,)),
            pltpu.SemaphoreType.REGULAR((3, 2)),
        ],
        compiler_params=pltpu.CompilerParams(
            collective_id=0, has_side_effects=True, vmem_limit_bytes=60 * 1024 * 1024
        ),
        name="sweep",
    )(factor, target_blocks, diag_inverse, cols, jnp.swapaxes(pair_list, 3, 4))


def solution(mesh):
    placed = (
        P("rows", None, None, None),
        P("rows", "inner", None, None),
        P("rows", None, None),
        P("rows", None),
        P(None, "rows", "inner", None, None),
    )
    return jax.shard_map(
        per_device,
        mesh=mesh,
        in_specs=placed,
        out_specs=P("rows", "inner", None, None),
        check_vma=False,
    )
```

```python
import jax
import jax.numpy as jnp
from jax import lax
from jax.experimental import pallas as pl
from jax.experimental.pallas import tpu as pltpu
from jax.sharding import PartitionSpec as P

MESH = pl.DeviceIdType.MESH
BAND = 16
BS = 128
GROUPS = 48
RING = 8
HOPS = 8
SLICE = 16
WINDOW = ((0, 2), (0, 8), (2, 5), (2, 4), (2, 3), (2, 1), (8, 6), (8, 7))
ENDS = ((40, 5, 7), (40, 5, 6), (41, 5, 6), (46, 0, 1))
ARRIVALS = tuple((m, q) for stage in ((2, 8), (1, 3, 7, 4, 5, 6)) for q in range(3) for m in stage)
HALF = BS // 2
KEPT = {0: 0, 2: 1, 6: 2}
ROUND = tuple(range(1, RING))


def kernel(
    factor, target, inverse, cols_in, pairs_in, out,
    left, own_0, own_1, slab, mate_0, mate_1, cols, pairs, mate_pairs, part, far, inv_out, inv_in, near, goal, kept, turned,
    local_sem, win_send, win_recv, end_send, mate_send, mate_recv, list_send, list_recv,
    sum_send, sum_recv, inv_send, inv_recv, greet,
):
    own, mate = (own_0, own_1), (mate_0, mate_1)
    group = lax.axis_index("rows")
    slot = lax.axis_index("inner")
    ring_at = slot // 2
    core = slot % 2
    other = slot + 1 - 2 * core
    first_row = group * 2 - BAND
    my_slice = pl.ds(pl.multiple_of(ring_at * SLICE, SLICE), SLICE)

    def along(step):
        return (lax.rem(group + step + GROUPS, GROUPS), slot)

    def around(step):
        return (group, lax.rem(ring_at + step + RING, RING) * 2 + core)

    sibling = (group, other)

    loads = [
        pltpu.make_async_copy(factor.at[:, slot, pl.ds(0, HALF)], own_0.at[0], local_sem.at[0]),
        pltpu.make_async_copy(factor.at[:, slot, pl.ds(HALF, HALF)], own_1.at[0], local_sem.at[1]),
        pltpu.make_async_copy(inverse.at[:, my_slice], slab.at[0], local_sem.at[2]),
        pltpu.make_async_copy(pairs_in, pairs, local_sem.at[3]),
        pltpu.make_async_copy(cols_in, cols, local_sem.at[4]),
        pltpu.make_async_copy(factor.at[:, other, pl.ds(0, HALF)], mate_0.at[0], local_sem.at[5]),
        pltpu.make_async_copy(factor.at[:, other, pl.ds(HALF, HALF)], mate_1.at[0], local_sem.at[6]),
        pltpu.make_async_copy(target, goal, local_sem.at[7]),
        pltpu.make_async_copy(factor, left, local_sem.at[8]),
    ]

    def remote(source, destination, send_sem, recv_sem, device):
        return pltpu.make_async_remote_copy(
            src_ref=source, dst_ref=destination, send_sem=send_sem, recv_sem=recv_sem,
            device_id=device, device_id_type=MESH,
        )

    def active(k, m):
        return jnp.logical_and(group >= k, group - k + max(k, m) < GROUPS)

    steps = {}
    for k, m in WINDOW:
        d = m - k
        sends = active(k, m)
        comes = jnp.logical_and(group >= m, group - m + max(k, m) < GROUPS)
        if d in steps:
            sends = jnp.logical_or(sends, steps[d][0])
            comes = jnp.logical_or(comes, steps[d][1])
        steps[d] = (sends, comes)
    for g, k, m in ENDS:
        d = m - k
        sends, comes = group == g + k, group == g + m
        if d in steps:
            sends = jnp.logical_or(sends, steps[d][0])
            comes = jnp.logical_or(comes, steps[d][1])
        steps[d] = (sends, comes)

    barrier = pltpu.get_barrier_semaphore()
    for step in (1, -1):
        pl.semaphore_signal(barrier, inc=1, device_id=around(step), device_id_type=MESH)
    pl.semaphore_signal(barrier, inc=1, device_id=sibling, device_id_type=MESH)
    partners = jnp.int32(3)
    for d, (sends, comes) in steps.items():
        @pl.when(comes)
        def _():
            pl.semaphore_signal(barrier, inc=1, device_id=along(-d), device_id_type=MESH)
        partners = partners + sends.astype(jnp.int32)
    for load in loads:
        load.start()
    for load in loads[:3]:
        load.wait()
    pl.semaphore_wait(barrier, partners)

    def piece(k, q):
        return slab.at[k, core] if q == 2 else own[q].at[k]

    def window_copy(k, m, q, send_sem):
        return remote(piece(k, q), piece(m, q), send_sem, win_recv.at[m - 1, q], along(m - k))

    def mate_copy(k, q):
        landing = piece(k, q) if q == 2 else mate[q].at[k]
        return remote(piece(k, q), landing, mate_send.at[k - 1, q], mate_recv.at[k - 1, q], sibling)

    def pass_on(held, q):
        for n, (k, m) in enumerate(WINDOW):
            if k == held:
                @pl.when(active(k, m))
                def _():
                    window_copy(k, m, q, win_send.at[n, q]).start()
        for n, (g, k, m) in enumerate(ENDS):
            if k == held:
                @pl.when(group == g + k)
                def _():
                    window_copy(k, m, q, end_send.at[n, q]).start()
        if held:
            mate_copy(held, q).start()

    list_copy = remote(pairs, mate_pairs, list_send.at[0], list_recv.at[0], sibling)

    def greeting(n):
        for way, step in enumerate((1, -1)):
            pl.semaphore_signal(greet.at[n, way], inc=1, device_id=around(step), device_id_type=MESH)

    def greeted(n):
        for way in range(2):
            pl.semaphore_wait(greet.at[n, way], 1)

    for q in range(3):
        pass_on(0, q)
    greeting(0)
    loads[3].wait()
    list_copy.start()

    def arrive(m, q):
        @pl.when(group >= m)
        def _():
            window_copy(0, m, q, win_send.at[0, q]).wait_recv()
            pass_on(m, q)

    def mates(q):
        for m in range(1, HOPS + 1):
            @pl.when(group >= m)
            def _():
                mate_copy(m, q).wait_recv()

    pending = list(ARRIVALS)

    def gather(upto):
        while pending:
            m, q = pending.pop(0)
            arrive(m, q)
            if (m, q) == upto:
                return

    for n in range(3):
        gather(ARRIVALS[3 * n + 2])
        greeted(n)
        if n < 2:
            greeting(n + 1)

    def locate(row, column):
        relative = cols[row, column] - first_row
        back = HOPS - lax.shift_right_arithmetic(relative, 1)
        return jnp.clip(back, 0, HOPS), relative & 1

    def partial_sums(e, q):
        column = lax.rem(ring_at + e, RING) * 2 + core
        totals = [jnp.zeros((HALF, BS), jnp.float32) for _ in range(2)]
        for table, window in ((pairs, own), (mate_pairs, mate)):
            for s in range(2):
                row = table[0, 0, 0, s, column]
                a = table[1, 0, 0, s, column]
                live = table[2, 0, 0, s, column]
                back, half = locate(row, column)
                product = lax.dot_general(
                    window[q][back, half], left[row, a],
                    (((1,), (1,)), ((), ())), preferred_element_type=jnp.float32,
                )
                for i in range(2):
                    wanted = jnp.logical_and(live == 1, row == i)
                    totals[i] = totals[i] + jnp.where(wanted, product, 0.0)
        return totals

    sent = []

    def hold(e, q):
        for i, total in enumerate(partial_sums(e, q)):
            part[q, e, i] = total.astype(jnp.bfloat16)

    def keep(e, q):
        for i, total in enumerate(partial_sums(e, q)):
            kept[q, KEPT[e], i] = total

    def sum_copy(n, q):
        source, destination, step = {
            0: (part.at[q, 3], near.at[q, 0], 1),
            1: (part.at[q, 5], near.at[q, 1], -1),
            2: (part.at[q, 4, 0], far.at[q, 0], -2),
            3: (part.at[q, 4, 1], far.at[q, 1], 2),
            4: (part.at[q, 1], near.at[q, 2], 1),
            5: (part.at[q, 7], near.at[q, 3], -1),
            6: (part.at[q, 2], near.at[q, 4], 2),
            7: (part.at[q, 6], near.at[q, 5], -2),
        }[n]
        return remote(source, destination, sum_send.at[n, q], sum_recv.at[n, q], around(step))

    def inverse_copy(e, place):
        return remote(inv_out.at[e], inv_in.at[:, place], inv_send.at[e - 1], inv_recv.at[e - 1], around(e))

    def send(copy):
        copy.start()
        sent.append(copy)

    def first_sums(q):
        hold(4, q)
        send(sum_copy(2, q))
        send(sum_copy(3, q))
        hold(3, q)
        send(sum_copy(0, q))
        hold(5, q)
        send(sum_copy(1, q))
        hold(1, q)
        send(sum_copy(4, q))
        hold(7, q)
        send(sum_copy(5, q))
        for e in (2, 6, 0):
            keep(e, q)

    def second_sums(q):
        for e, n, first, second, extra in ((2, 6, 0, 3, 1), (6, 7, 1, 2, 0)):
            sum_copy(first, q).wait_recv()
            sum_copy(second, q).wait_recv()
            for i in range(2):
                total = kept[q, KEPT[e], i] + near[q, first, i].astype(jnp.float32)
                if i == extra:
                    total = total + far[q, extra].astype(jnp.float32)
                part[q, e, i] = total.astype(jnp.bfloat16)
            send(sum_copy(n, q))

    def last_sums(q):
        totals = [kept[q, 0, i] for i in range(2)]
        for n in (4, 5, 6, 7):
            sum_copy(n, q).wait_recv()
            for i in range(2):
                totals[i] = totals[i] + near[q, n - 2, i].astype(jnp.float32)
        results = []
        for i in range(2):
            rows = pl.ds(q * HALF, HALF)
            difference = (turned[i, rows] - totals[i]).astype(jnp.bfloat16)
            results.append(lax.dot_general(
                difference, inv_in[i, rows], (((0,), (0,)), ((), ())), preferred_element_type=jnp.float32
            ))
        return results

    gather((6, 0))
    for load in loads[4:]:
        load.wait()
    list_copy.wait_recv()
    for i in range(2):
        turned[i] = goal[i, 0].astype(jnp.float32).T
    mates(0)
    first_sums(0)
    gather((6, 1))
    mates(1)
    first_sums(1)
    gather(None)
    second_sums(0)
    mates(2)
    for e in (4, 3, 5, 0):
        column = lax.rem(ring_at + e, RING) * 2 + core
        for i in range(2):
            back, half = locate(i, column)
            inv_out[e, i] = slab[back, half]
        if e:
            send(inverse_copy(e, my_slice))
    inv_in[:, my_slice, :] = inv_out[0]
    list_copy.wait_send()
    for q in range(3):
        for n, (k, m) in enumerate(WINDOW):
            @pl.when(active(k, m))
            def _():
                window_copy(k, m, q, win_send.at[n, q]).wait_send()
        for n, (g, k, m) in enumerate(ENDS):
            @pl.when(group == g + k)
            def _():
                window_copy(k, m, q, end_send.at[n, q]).wait_send()
        for m in range(1, HOPS + 1):
            @pl.when(group >= m)
            def _():
                mate_copy(m, q).wait_send()
    second_sums(1)
    for e in (2, 6, 1, 7):
        column = lax.rem(ring_at + e, RING) * 2 + core
        for i in range(2):
            back, half = locate(i, column)
            inv_out[e, i] = slab[back, half]
        if e:
            send(inverse_copy(e, my_slice))
    for e in ROUND:
        start = lax.rem(ring_at - e + RING, RING) * SLICE
        inverse_copy(e, pl.ds(pl.multiple_of(start, SLICE), SLICE)).wait_recv()
    last = sent[-6:]
    for copy in sent[:-6]:
        copy.wait_send()
    lower = last_sums(0)
    upper = last_sums(1)
    for i in range(2):
        result = jnp.where(cols[i, slot] < 0, 0.0, lower[i] + upper[i])
        out[i, 0] = result.astype(jnp.bfloat16)

    for copy in last:
        copy.wait_send()


def per_device(factor, target_blocks, diag_inverse, cols, pair_list):
    bf16 = jnp.bfloat16
    anywhere = pl.BlockSpec(memory_space=pltpu.HBM)
    dma = pltpu.SemaphoreType.DMA
    return pl.pallas_call(
        kernel,
        out_shape=jax.ShapeDtypeStruct((2, 1, BS, BS), bf16),
        in_specs=[anywhere] * 5,
        out_specs=pl.BlockSpec(memory_space=pltpu.VMEM),
        scratch_shapes=[
            pltpu.VMEM((2, 16, BS, BS), bf16),
            pltpu.VMEM((HOPS + 1, 2, HALF, BS), bf16),
            pltpu.VMEM((HOPS + 1, 2, HALF, BS), bf16),
            pltpu.VMEM((HOPS + 1, 2, SLICE, BS), bf16),
            pltpu.VMEM((HOPS + 1, 2, HALF, BS), bf16),
            pltpu.VMEM((HOPS + 1, 2, HALF, BS), bf16),
            pltpu.SMEM((2, 16), jnp.int32),
            pltpu.SMEM((3, 1, 1, 2, 16), jnp.int32),
            pltpu.SMEM((3, 1, 1, 2, 16), jnp.int32),
            pltpu.VMEM((2, RING, 2, HALF, BS), bf16),
            pltpu.VMEM((2, 2, HALF, BS), bf16),
            pltpu.VMEM((RING, 2, SLICE, BS), bf16),
            pltpu.VMEM((2, BS, BS), bf16),
            pltpu.VMEM((2, 6, 2, HALF, BS), bf16),
            pltpu.VMEM((2, 1, BS, BS), bf16),
            pltpu.VMEM((2, 3, 2, HALF, BS), jnp.float32),
            pltpu.VMEM((2, BS, BS), jnp.float32),
            dma((9,)),
            dma((len(WINDOW), 3)),
            dma((HOPS, 3)),
            dma((len(ENDS), 3)),
            dma((HOPS, 3)),
            dma((HOPS, 3)),
            dma((1,)),
            dma((1,)),
            dma((8, 2)),
            dma((8, 2)),
            dma((RING - 1,)),
            dma((RING - 1,)),
            pltpu.SemaphoreType.REGULAR((3, 2)),
        ],
        compiler_params=pltpu.CompilerParams(
            collective_id=0, has_side_effects=True, vmem_limit_bytes=60 * 1024 * 1024
        ),
        name="sweep",
    )(factor, target_blocks, diag_inverse, cols, jnp.swapaxes(pair_list, 3, 4))


def solution(mesh):
    placed = (
        P("rows", None, None, None),
        P("rows", "inner", None, None),
        P("rows", None, None),
        P("rows", None),
        P(None, "rows", "inner", None, None),
    )
    return jax.shard_map(
        per_device,
        mesh=mesh,
        in_specs=placed,
        out_specs=P("rows", "inner", None, None),
        check_vma=False,
    )
```
